32 devices in a mesh: rep: 8 (over y, x, core), shard: 4 (over z).
Axes of the slice: x: 2, y: 2, z: 4, core: 2. Of those that a mesh axis runs over, the one named last changes fastest.
Arguments:
- tokens: bfloat16 [4096, 4608], P(('rep', 'shard')), may hold values from -384 to 384
- key_cot: bfloat16 [4096, 1024], P(('rep', 'shard')), may hold values from -6 to 6
- norm_gain: float32 [4608], replicated, may hold values from 0.5 to 1.5
- key_weight: bfloat16 [4608, 1024], P('shard'), may hold values from -0.09375 to 0.09375
- codes_m: int32 [4608, 1024], P('shard'), may hold values from 0 to 255
- codes_v: int32 [4608, 1024], P('shard'), may hold values from 0 to 255
- scale_m: float32 [2304], P('shard'), may hold values from 19.2 to 192
- scale_v: float32 [2304], P('shard'), may hold values from 409.6 to 8192
- qmap_m: float32 [256], replicated, may hold values from -1 to 1, as said below
- qmap_v: float32 [256], replicated, may hold values from 0.01 to 1, as said below
Outputs:
- input_grad: bfloat16 [4096, 4608], P(('rep', 'shard'))
- gain_grad: float32 [4608], replicated
- new_weight: bfloat16 [4608, 1024], P('shard')
- new_scale_m: float32 [2304], P('shard')
- new_scale_v: float32 [2304], P('shard')
The draws below stay inside these ranges and needn't reach their ends.
Inputs may be any that keep to these rules, and one draw needn't show every extreme that they name: `qmap_m`: entries rise with the index. `qmap_v`: entries rise with the index.
All inputs are finite; a program needn't handle non-finite values.
Results may differ from the reference program's by a relative error of at most 0.0095.
Values may be sent and summed in bfloat16 or wider, within the bound.
A program may use at most 128 MiB of HBM per device.

```python
import math
import jax
import jax.numpy as jnp
from jax import lax

D = 4608
KD = 1024
TOK_DEV = 128
BLOCK = 2048
CODES = 256
TOKENS = 4096
BLOCKS = 2304
N_REP = 8
N_SHARD = 4


def draw_tokens(key, part):
    key_base, key_lift, key_owner = jax.random.split(key, 3)
    devices = TOKENS // TOK_DEV
    base = jax.random.normal(key_base, (TOKENS, D))
    lift = jnp.exp(jax.random.uniform(key_lift, (TOKENS, 1)) * math.log(10.0))
    base = jnp.clip(base, -4.0, 4.0)
    owner = jax.random.permutation(key_owner, devices)
    row_device = lax.broadcasted_iota(jnp.int32, (TOKENS, D), 0) // TOK_DEV
    col_block = lax.broadcasted_iota(jnp.int32, (TOKENS, D), 1) // (D // devices)
    spike = jnp.where(col_block == owner[row_device], 6.0, 1.0)
    return (base * lift * spike).astype(jnp.bfloat16)


def draw_qmap_m(key, part):
    raw = jax.random.uniform(key, (CODES,), minval=-1.0, maxval=1.0)
    return jnp.sort(raw).astype(jnp.float32)


def draw_qmap_v(key, part):
    raw = jnp.exp(jax.random.uniform(key, (CODES,), minval=math.log(0.01), maxval=0.0))
    return jnp.clip(jnp.sort(raw), 0.01, 1.0).astype(jnp.float32)


def set_ends(array, own_key, low, top_value):
    shape = array.shape
    place = [jax.random.randint(jax.random.fold_in(own_key, axis), (), 0, shape[axis]) for axis in range(len(shape))]
    array = array.at[tuple(place)].set(low)
    longest = shape.index(max(shape))
    place[longest] = (place[longest] + 1) % shape[longest]
    return array.at[tuple(place)].set(top_value)


def level_of(key, shape, shards, smallest, top_value):
    def one(position, blocks):
        draws = jax.random.uniform(jax.random.fold_in(jax.random.fold_in(key, 6), position), (blocks,), jnp.float32, smallest / len(shards), top_value / len(shards))
        return jnp.repeat(jnp.exp(draws), shape[position] // blocks).reshape((-1,) + (1,) * (len(shape) - position - 1))

    level = one(*shards[0])
    for cut in shards[1:]:
        level = level * one(*cut)
    return level


def scatter_about(own_key, dims, deviation, reach, cuts=(), kind=jnp.bfloat16):
    result = deviation * jax.random.normal(own_key, dims, jnp.float32)
    if cuts:
        result = result * level_of(own_key, dims, cuts, -0.22, 0.18)
    return jnp.clip(result, -reach, reach).astype(kind)


def setup_inputs(seed: int = 0) -> dict:
    streams_of = jax.random.split(jax.random.key(seed), 11)
    tokens = draw_tokens(jax.random.fold_in(streams_of[10], 71), 0)
    key_cot = scatter_about(streams_of[1], (TOKENS, KD), 1.0, 6.0, ((0, 32),))
    norm_gain = jnp.clip(1.0 + 0.1 * jax.random.normal(streams_of[2], (D,), jnp.float32), 0.5, 1.5)
    key_weight = scatter_about(streams_of[3], (D, KD), D ** -0.5, 0.09375, ((0, 4),))
    codes_m = set_ends(jax.random.randint(streams_of[4], (D, KD), 0, CODES), jax.random.fold_in(streams_of[4], 1), 0, CODES - 1).astype(jnp.int32)
    codes_v = set_ends(jax.random.randint(streams_of[5], (D, KD), 0, CODES), jax.random.fold_in(streams_of[5], 1), 0, CODES - 1).astype(jnp.int32)
    scale_m = jnp.clip(jnp.exp(math.log(192.0) - 2.3025851 * jax.random.uniform(streams_of[6], (BLOCKS,), jnp.float32) ** level_of(streams_of[6], (BLOCKS,), ((0, 4),), -0.2, 0.2)), 19.2, 192.0)
    scale_v = jnp.clip(jnp.exp(math.log(8192.0) - 2.9957323 * jax.random.uniform(streams_of[7], (BLOCKS,), jnp.float32) ** level_of(streams_of[7], (BLOCKS,), ((0, 4),), -0.2, 0.2)), 409.6, 8192.0)
    qmap_m = draw_qmap_m(jax.random.fold_in(streams_of[10], 71), 0)
    qmap_v = draw_qmap_v(jax.random.fold_in(streams_of[10], 71), 0)
    return {"tokens": tokens, "key_cot": key_cot, "norm_gain": norm_gain, "key_weight": key_weight, "codes_m": codes_m, "codes_v": codes_v, "scale_m": scale_m, "scale_v": scale_v, "qmap_m": qmap_m, "qmap_v": qmap_v}


eps_norm = 1e-06
beta_one = 0.9
beta_two = 0.95
adam_eps = 1e-08
learn_rate = 0.01
decay_rate = 0.1
bias_one = 1.0 - 0.9 ** 10
bias_two = 1.0 - 0.95 ** 10

def normalize(tokens, norm_gain):
    wide = tokens.astype(jnp.float32)
    inv_rms = lax.rsqrt(lax.optimization_barrier(jnp.mean(wide * wide, axis=-1, keepdims=True)) + eps_norm)
    normed = (wide * inv_rms * norm_gain.astype(jnp.float32)).astype(jnp.bfloat16)
    return (wide, inv_rms, normed)

def norm_backward(wide, inv_rms, norm_gain, normed_grad):
    scaled = normed_grad * norm_gain.astype(jnp.float32)
    inner = lax.optimization_barrier(jnp.mean(scaled * wide, axis=-1, keepdims=True))
    input_grad = (inv_rms * scaled - wide * inv_rms ** 3 * inner).astype(jnp.bfloat16)
    gain_term = lax.optimization_barrier(jnp.sum(normed_grad * wide * inv_rms, axis=0))
    return (input_grad, gain_term)

def rounded(value):
    lowered = lax.optimization_barrier(value.astype(jnp.bfloat16))
    return lowered.astype(jnp.float32)

def adam_update(weight, grad, old_m, old_v):
    first = beta_one * old_m + (1.0 - beta_one) * grad
    second = beta_two * old_v + (1.0 - beta_two) * grad * grad
    direction = first / bias_one / (jnp.sqrt(second / bias_two) + adam_eps)
    new_weight = (weight.astype(jnp.float32) * (1.0 - learn_rate * decay_rate) - learn_rate * direction).astype(jnp.bfloat16)
    return (new_weight, first, second)

def block_max(values, row_group):
    blocks = values.reshape(values.shape[0] // row_group, -1)
    return lax.optimization_barrier(jnp.max(jnp.abs(blocks), axis=1))

def reference(tokens, key_cot, norm_gain, key_weight, codes_m, codes_v, scale_m, scale_v, qmap_m, qmap_v):
    devices = N_REP * N_SHARD
    token_blocks = tokens.reshape(devices, TOK_DEV, D)
    cot_blocks = key_cot.reshape(devices, TOK_DEV, KD)

    def one_device(carry, block_pair):
        grad_total, gain_total = carry
        block_tokens, block_cot = block_pair
        wide, inv_rms, normed = normalize(block_tokens, norm_gain)
        normed_grad = jnp.dot(block_cot, key_weight.T, preferred_element_type=jnp.float32)
        input_grad, gain_term = norm_backward(wide, inv_rms, norm_gain, normed_grad)
        term = rounded(jnp.dot(normed.T, block_cot, preferred_element_type=jnp.float32))
        return ((grad_total + term, gain_total + gain_term), input_grad)
    start_carry = (jnp.zeros((D, KD), jnp.float32), jnp.zeros((D,), jnp.float32))
    (grad, gain_grad), block_grads = lax.scan(one_device, start_carry, (token_blocks, cot_blocks))
    input_grad = block_grads.reshape(TOKENS, D)
    row_group = BLOCK // KD
    old_m = qmap_m[codes_m] * jnp.repeat(scale_m, row_group)[:, None]
    old_v = qmap_v[codes_v] * jnp.repeat(scale_v, row_group)[:, None]
    new_weight, first, second = adam_update(key_weight, grad, old_m, old_v)
    return (input_grad, gain_grad, new_weight, block_max(first, row_group), block_max(second, row_group))
```

```python
import math

import jax
import jax.numpy as jnp
from jax import lax
from jax.experimental import pallas as pl
from jax.experimental.pallas import tpu as pltpu
from jax.sharding import PartitionSpec as P

BLOCK = 2048


eps_norm = 1e-06
beta_one = 0.9
beta_two = 0.95
adam_eps = 1e-08
learn_rate = 0.01
decay_rate = 0.1
bias_one = 1.0 - 0.9**10
bias_two = 1.0 - 0.95**10


def normalize(tokens, norm_gain):
    wide = tokens.astype(jnp.float32)
    inv_rms = lax.rsqrt(jnp.mean(wide * wide, axis=-1, keepdims=True) + eps_norm)
    normed = (wide * inv_rms * norm_gain).astype(jnp.bfloat16)
    return (wide, inv_rms, normed)


def norm_backward(wide, inv_rms, norm_gain, normed_grad):
    scaled = normed_grad * norm_gain
    inner = jnp.mean(scaled * wide, axis=-1, keepdims=True)
    input_grad = (inv_rms * scaled - wide * inv_rms**3 * inner).astype(jnp.bfloat16)
    gain_term = jnp.sum(normed_grad * wide * inv_rms, axis=0)
    return (input_grad, gain_term)


def rounded(value):
    lowered = lax.optimization_barrier(value.astype(jnp.bfloat16))
    return lowered.astype(jnp.float32)


def decode(codes, table):
    high_part = codes // 16
    low_part = codes - high_part * 16
    levels = lax.broadcasted_iota(jnp.int32, (16, 1, 1), 0)
    pick_low = (low_part[None] == levels).astype(jnp.float32)
    pick_high = (high_part[None] == levels).astype(jnp.float32)
    table_grid = table.reshape(16, 16)
    by_high = jnp.einsum("hl,lrk->hrk", table_grid, pick_low, precision=lax.Precision.HIGHEST)
    return jnp.sum(pick_high * by_high, axis=0)


def adam_update(weight, grad, old_m, old_v):
    first = beta_one * old_m + (1.0 - beta_one) * grad
    second = beta_two * old_v + (1.0 - beta_two) * grad * grad
    direction = first / bias_one / (jnp.sqrt(second / bias_two) + adam_eps)
    new_weight = (
        weight.astype(jnp.float32) * (1.0 - learn_rate * decay_rate) - learn_rate * direction
    ).astype(jnp.bfloat16)
    return (new_weight, first, second)


def block_max(values, row_group):
    blocks = values.reshape(values.shape[0] // row_group, -1)
    return jnp.max(jnp.abs(blocks), axis=1)


def optimize(
    weight, grad, codes_first, codes_second, scales_first, scales_second, qmap_m, qmap_v, row_group
):
    rows, width = weight.shape
    span_rows = math.gcd(rows, 64)
    span_count = rows // span_rows
    per_span = span_rows // row_group

    def one_span(pieces):
        weight_part, grad_part, code_one, code_two, scale_one, scale_two = pieces
        old_m = (
            decode(code_one, qmap_m).reshape(per_span, row_group, width) * scale_one[:, None, None]
        ).reshape(span_rows, width)
        old_v = (
            decode(code_two, qmap_v).reshape(per_span, row_group, width) * scale_two[:, None, None]
        ).reshape(span_rows, width)
        new_part, first, second = adam_update(weight_part, grad_part, old_m, old_v)
        return (new_part, block_max(first, row_group), block_max(second, row_group))

    pieces = (
        weight.reshape(span_count, span_rows, width),
        grad.reshape(span_count, span_rows, width),
        codes_first.reshape(span_count, span_rows, width),
        codes_second.reshape(span_count, span_rows, width),
        scales_first.reshape(span_count, per_span),
        scales_second.reshape(span_count, per_span),
    )
    new_weight, new_first, new_second = lax.map(one_span, pieces)
    return (new_weight.reshape(rows, width), new_first.reshape(-1), new_second.reshape(-1))


def plain_shards(
    tokens, key_cot, norm_gain, key_weight, codes_m, codes_v, scale_m, scale_v, qmap_m, qmap_v
):
    width = key_cot.shape[1]
    row_group = BLOCK // width
    wide, inv_rms, normed = normalize(tokens, norm_gain)
    group_cot = lax.all_gather(key_cot, "shard", axis=0, tiled=True)
    local_cols = jnp.einsum("tk,dk->td", group_cot, key_weight, preferred_element_type=jnp.float32)
    normed_grad = lax.all_to_all(local_cols, "shard", split_axis=0, concat_axis=1, tiled=True)
    input_grad, gain_term = norm_backward(wide, inv_rms, norm_gain, normed_grad)
    gain_grad = lax.psum(gain_term, ("rep", "shard"))
    shard_count = lax.axis_size("shard")
    rep_count = lax.axis_size("rep")
    slice_rows = key_weight.shape[0] // rep_count
    reordered = normed.reshape(normed.shape[0], shard_count, rep_count, slice_rows)
    reordered = reordered.transpose(0, 2, 1, 3).reshape(normed.shape)
    grad = lax.psum_scatter(
        rounded(jnp.einsum("td,tk->dk", reordered, key_cot, preferred_element_type=jnp.float32)),
        ("rep", "shard"),
        scatter_dimension=0,
        tiled=True,
    )
    first_row = lax.axis_index("rep") * slice_rows
    first_block = lax.axis_index("rep") * (slice_rows // row_group)

    def take_rows(array_in):
        return lax.dynamic_slice_in_dim(array_in, first_row, slice_rows, 0)

    def take_blocks(array_in):
        return lax.dynamic_slice_in_dim(array_in, first_block, slice_rows // row_group, 0)

    part_weight, part_m, part_v = optimize(
        take_rows(key_weight),
        grad,
        take_rows(codes_m),
        take_rows(codes_v),
        take_blocks(scale_m),
        take_blocks(scale_v),
        qmap_m,
        qmap_v,
        row_group,
    )
    new_weight = lax.all_gather(part_weight, "rep", axis=0, tiled=True)
    new_scale_m, new_scale_v = (
        lax.all_gather(part_m, "rep", axis=0, tiled=True),
        lax.all_gather(part_v, "rep", axis=0, tiled=True),
    )
    return (input_grad, gain_grad, new_weight, new_scale_m, new_scale_v)


def lookup(codes, table):
    low = codes & 127
    first = jnp.take_along_axis(table[0], low, axis=1)
    second = jnp.take_along_axis(table[1], low, axis=1)
    return jnp.where(codes >= 128, second, first)


def decode_kernel(rows, qm_ref, qv_ref, sm_ref, sv_ref, cm_hbm, cv_hbm, old_m, old_v, cm, cv, sems):
    start = pl.multiple_of(lax.axis_index("rep") * rows, 8)
    copies = [
        pltpu.make_async_copy(src.at[pl.ds(start, rows)], dst, sems.at[i])
        for i, (src, dst) in enumerate(((cm_hbm, cm), (cv_hbm, cv)))
    ]
    for copy in copies:
        copy.start()
    for copy, codes, table_ref, scale, out in (
        (copies[0], cm, qm_ref, sm_ref, old_m),
        (copies[1], cv, qv_ref, sv_ref, old_v),
    ):
        copy.wait()
        tables = [jnp.broadcast_to(table_ref[i : i + 1, :], (8, 128)) for i in range(2)]

        @pl.loop(0, rows // 8)
        def _(step):
            row = pl.multiple_of(step * 8, 8)
            factor = scale[pl.ds(row, 8), :]
            for col in range(0, codes.shape[1], 128):
                value = lookup(codes[pl.ds(row, 8), col : col + 128], tables)
                out[pl.ds(row, 8), col : col + 128] = value * factor


def decode_rows(codes_m, codes_v, scale_m, scale_v, qmap_m, qmap_v, rows, row_group):
    width = codes_m.shape[1]
    first_block = lax.axis_index("rep") * (rows // row_group)

    def spread(scale):
        mine = lax.dynamic_slice_in_dim(scale, first_block, rows // row_group, 0)
        return jnp.broadcast_to(jnp.repeat(mine, row_group)[:, None], (rows, 128))

    vmem = pl.BlockSpec(memory_space=pltpu.VMEM)
    anywhere = pl.BlockSpec(memory_space=pl.ANY)
    shape = jax.ShapeDtypeStruct((rows, width), jnp.float32)
    return pl.pallas_call(
        lambda *refs: decode_kernel(rows, *refs),
        out_shape=(shape, shape),
        in_specs=[vmem] * 4 + [anywhere] * 2,
        out_specs=(vmem, vmem),
        scratch_shapes=[
            pltpu.VMEM((rows, width), jnp.int32),
            pltpu.VMEM((rows, width), jnp.int32),
            pltpu.SemaphoreType.DMA((2,)),
        ],
        compiler_params=pltpu.CompilerParams(vmem_limit_bytes=16 * 2**20),
        name="decode",
    )(qmap_m.reshape(2, 128), qmap_v.reshape(2, 128), spread(scale_m), spread(scale_v), codes_m, codes_v)


def tiled_shards(
    tokens, key_cot, norm_gain, key_weight, codes_m, codes_v, scale_m, scale_v, qmap_m, qmap_v
):
    row_group = BLOCK // key_cot.shape[1]
    features = tokens.shape[1]
    rows = key_weight.shape[0]
    slice_rows = rows // lax.axis_size("rep")
    rep, shard = lax.axis_index("rep"), lax.axis_index("shard")
    old_m, old_v = decode_rows(
        codes_m, codes_v, scale_m, scale_v, qmap_m, qmap_v, slice_rows, row_group
    )
    wide = tokens.astype(jnp.float32)
    inv_rms = lax.rsqrt(jnp.mean(wide * wide, axis=-1, keepdims=True) + eps_norm)
    scaled_cot = (key_cot.astype(jnp.float32) * inv_rms).astype(jnp.bfloat16)
    group_cot = lax.all_gather(scaled_cot, "shard", axis=0, tiled=True)
    group_tokens = lax.all_to_all(tokens, "shard", split_axis=1, concat_axis=0, tiled=True)
    cols = jnp.einsum("tk,dk->td", group_cot, key_weight, preferred_element_type=jnp.float32)
    home = lax.all_to_all(
        cols.astype(jnp.bfloat16), "shard", split_axis=0, concat_axis=1, tiled=True
    ).astype(jnp.float32)
    gain_term = lax.psum(jnp.sum(cols * group_tokens.astype(jnp.float32), axis=0), "rep")
    gain_grad = lax.all_gather(gain_term, "shard", axis=0, tiled=True)
    scaled = home * norm_gain
    inner = jnp.sum(scaled * wide, axis=-1, keepdims=True) * (1.0 / features)
    input_grad = (scaled - wide * (inv_rms * inv_rms * inner)).astype(jnp.bfloat16)
    my_gain = lax.dynamic_slice_in_dim(norm_gain, shard * rows, rows, 0)
    partial = jnp.einsum(
        "td,tk->dk", group_tokens, group_cot, preferred_element_type=jnp.float32
    ) * my_gain[:, None]
    grad = lax.psum_scatter(
        partial.astype(jnp.bfloat16), "rep", scatter_dimension=0, tiled=True
    ).astype(jnp.float32)
    my_weight = lax.dynamic_slice_in_dim(key_weight, rep * slice_rows, slice_rows, 0)
    part_weight, first, second = adam_update(my_weight, grad, old_m, old_v)
    new_weight = lax.all_gather(part_weight, "rep", axis=0, tiled=True)
    maxima = jnp.stack([block_max(first, row_group), block_max(second, row_group)])
    maxima = lax.all_gather(maxima, "rep", axis=1, tiled=True)
    return (input_grad, gain_grad, new_weight, maxima[0], maxima[1])


def shards(tokens, key_cot, norm_gain, key_weight, *rest):
    slice_rows = key_weight.shape[0] // lax.axis_size("rep")
    even = slice_rows % 16 == 0 and key_weight.shape[0] % 128 == 0
    body = tiled_shards if even else plain_shards
    return body(tokens, key_cot, norm_gain, key_weight, *rest)


def solution(mesh):
    placed = (
        P(("rep", "shard"), None),
        P(("rep", "shard"), None),
        P(),
        P("shard", None),
        P("shard", None),
        P("shard", None),
        P("shard"),
        P("shard"),
        P(),
        P(),
    )
    return jax.shard_map(
        shards,
        mesh=mesh,
        in_specs=placed,
        out_specs=(P(("rep", "shard"), None), P(), P("shard", None), P("shard"), P("shard")),
        check_vma=False,
    )
```

```python
import math

import jax
import jax.numpy as jnp
from jax import lax
from jax.experimental import pallas as pl
from jax.experimental.pallas import tpu as pltpu
from jax.sharding import PartitionSpec as P

BLOCK = 2048
CHUNKS = 3
MESH = pl.DeviceIdType.MESH


eps_norm = 1e-06
beta_one = 0.9
beta_two = 0.95
adam_eps = 1e-08
learn_rate = 0.01
decay_rate = 0.1
bias_one = 1.0 - 0.9**10
bias_two = 1.0 - 0.95**10


def normalize(tokens, norm_gain):
    wide = tokens.astype(jnp.float32)
    inv_rms = lax.rsqrt(jnp.mean(wide * wide, axis=-1, keepdims=True) + eps_norm)
    normed = (wide * inv_rms * norm_gain).astype(jnp.bfloat16)
    return (wide, inv_rms, normed)


def norm_backward(wide, inv_rms, norm_gain, normed_grad):
    scaled = normed_grad * norm_gain
    inner = jnp.mean(scaled * wide, axis=-1, keepdims=True)
    input_grad = (inv_rms * scaled - wide * inv_rms**3 * inner).astype(jnp.bfloat16)
    gain_term = jnp.sum(normed_grad * wide * inv_rms, axis=0)
    return (input_grad, gain_term)


def rounded(value):
    lowered = lax.optimization_barrier(value.astype(jnp.bfloat16))
    return lowered.astype(jnp.float32)


def decode(codes, table):
    high_part = codes // 16
    low_part = codes - high_part * 16
    levels = lax.broadcasted_iota(jnp.int32, (16, 1, 1), 0)
    pick_low = (low_part[None] == levels).astype(jnp.float32)
    pick_high = (high_part[None] == levels).astype(jnp.float32)
    table_grid = table.reshape(16, 16)
    by_high = jnp.einsum("hl,lrk->hrk", table_grid, pick_low, precision=lax.Precision.HIGHEST)
    return jnp.sum(pick_high * by_high, axis=0)


def adam_update(weight, grad, old_m, old_v):
    first = beta_one * old_m + (1.0 - beta_one) * grad
    second = beta_two * old_v + (1.0 - beta_two) * grad * grad
    direction = first / bias_one / (jnp.sqrt(second / bias_two) + adam_eps)
    new_weight = (
        weight.astype(jnp.float32) * (1.0 - learn_rate * decay_rate) - learn_rate * direction
    ).astype(jnp.bfloat16)
    return (new_weight, first, second)


def block_max(values, row_group):
    blocks = values.reshape(values.shape[0] // row_group, -1)
    return jnp.max(jnp.abs(blocks), axis=1)


def optimize(
    weight, grad, codes_first, codes_second, scales_first, scales_second, qmap_m, qmap_v, row_group
):
    rows, width = weight.shape
    span_rows = math.gcd(rows, 64)
    span_count = rows // span_rows
    per_span = span_rows // row_group

    def one_span(pieces):
        weight_part, grad_part, code_one, code_two, scale_one, scale_two = pieces
        old_m = (
            decode(code_one, qmap_m).reshape(per_span, row_group, width) * scale_one[:, None, None]
        ).reshape(span_rows, width)
        old_v = (
            decode(code_two, qmap_v).reshape(per_span, row_group, width) * scale_two[:, None, None]
        ).reshape(span_rows, width)
        new_part, first, second = adam_update(weight_part, grad_part, old_m, old_v)
        return (new_part, block_max(first, row_group), block_max(second, row_group))

    pieces = (
        weight.reshape(span_count, span_rows, width),
        grad.reshape(span_count, span_rows, width),
        codes_first.reshape(span_count, span_rows, width),
        codes_second.reshape(span_count, span_rows, width),
        scales_first.reshape(span_count, per_span),
        scales_second.reshape(span_count, per_span),
    )
    new_weight, new_first, new_second = lax.map(one_span, pieces)
    return (new_weight.reshape(rows, width), new_first.reshape(-1), new_second.reshape(-1))


def plain_shards(
    tokens, key_cot, norm_gain, key_weight, codes_m, codes_v, scale_m, scale_v, qmap_m, qmap_v
):
    width = key_cot.shape[1]
    row_group = BLOCK // width
    wide, inv_rms, normed = normalize(tokens, norm_gain)
    group_cot = lax.all_gather(key_cot, "shard", axis=0, tiled=True)
    local_cols = jnp.einsum("tk,dk->td", group_cot, key_weight, preferred_element_type=jnp.float32)
    normed_grad = lax.all_to_all(local_cols, "shard", split_axis=0, concat_axis=1, tiled=True)
    input_grad, gain_term = norm_backward(wide, inv_rms, norm_gain, normed_grad)
    gain_grad = lax.psum(gain_term, ("rep", "shard"))
    shard_count = lax.axis_size("shard")
    rep_count = lax.axis_size("rep")
    slice_rows = key_weight.shape[0] // rep_count
    reordered = normed.reshape(normed.shape[0], shard_count, rep_count, slice_rows)
    reordered = reordered.transpose(0, 2, 1, 3).reshape(normed.shape)
    grad = lax.psum_scatter(
        rounded(jnp.einsum("td,tk->dk", reordered, key_cot, preferred_element_type=jnp.float32)),
        ("rep", "shard"),
        scatter_dimension=0,
        tiled=True,
    )
    first_row = lax.axis_index("rep") * slice_rows
    first_block = lax.axis_index("rep") * (slice_rows // row_group)

    def take_rows(array_in):
        return lax.dynamic_slice_in_dim(array_in, first_row, slice_rows, 0)

    def take_blocks(array_in):
        return lax.dynamic_slice_in_dim(array_in, first_block, slice_rows // row_group, 0)

    part_weight, part_m, part_v = optimize(
        take_rows(key_weight),
        grad,
        take_rows(codes_m),
        take_rows(codes_v),
        take_blocks(scale_m),
        take_blocks(scale_v),
        qmap_m,
        qmap_v,
        row_group,
    )
    new_weight = lax.all_gather(part_weight, "rep", axis=0, tiled=True)
    new_scale_m, new_scale_v = (
        lax.all_gather(part_m, "rep", axis=0, tiled=True),
        lax.all_gather(part_v, "rep", axis=0, tiled=True),
    )
    return (input_grad, gain_grad, new_weight, new_scale_m, new_scale_v)


def lookup(codes, table):
    low = codes & 127
    first = jnp.take_along_axis(table[0], low, axis=1)
    second = jnp.take_along_axis(table[1], low, axis=1)
    return jnp.where(codes >= 128, second, first)


def decode_kernel(
    chunks, chunk_rows, part, qm_ref, qv_ref, sm_ref, sv_ref, cm_hbm, cv_hbm, old_m, old_v, cm, cv, sems
):
    rows = chunks * part
    copies = []
    for i, (src, dst) in enumerate(((cm_hbm, cm), (cv_hbm, cv))):
        for c in range(chunks):
            start = pl.multiple_of(c * chunk_rows + lax.axis_index("rep") * part, 8)
            copies.append(
                pltpu.make_async_copy(
                    src.at[pl.ds(start, part)], dst.at[pl.ds(c * part, part)], sems.at[i, c]
                )
            )
    for copy in copies:
        copy.start()
    for waits, codes, table_ref, scale, out in (
        (copies[:chunks], cm, qm_ref, sm_ref, old_m),
        (copies[chunks:], cv, qv_ref, sv_ref, old_v),
    ):
        for copy in waits:
            copy.wait()
        tables = [jnp.broadcast_to(table_ref[i : i + 1, :], (8, 128)) for i in range(2)]

        @pl.loop(0, rows // 8)
        def _(step):
            row = pl.multiple_of(step * 8, 8)
            factor = scale[pl.ds(row, 8), :]
            for col in range(0, codes.shape[1], 128):
                value = lookup(codes[pl.ds(row, 8), col : col + 128], tables)
                out[pl.ds(row, 8), col : col + 128] = value * factor


def fused_kernel(
    nr,
    ns,
    tok_hbm,
    cot_ref,
    gain_ref,
    gain_rows,
    w_hbm,
    old_m,
    old_v,
    ig_ref,
    nw_hbm,
    gain_out,
    scale_out,
    tok_v,
    w_v,
    tok_g,
    cot_g,
    ng,
    ng_home,
    part,
    core_recv,
    red,
    chip_recv,
    nw_own,
    inv_ref,
    gain_own,
    gain_recv,
    gain_sum,
    gain_z,
    scale_own,
    scale_recv,
    loc,
    cot_sem,
    tok_sem,
    ng_sem,
    core_sem,
    chip_sem,
    ag_sem,
    fwd_sem,
    gain_sem,
    gz_sem,
    scale_sem,
):
    rep, shard = lax.axis_index("rep"), lax.axis_index("shard")
    chips = nr // 2
    chip, core = rep // 2, rep % 2
    partner = rep + 1 - 2 * core
    count, features = tok_v.shape
    rows, width = w_v.shape
    span = rows // CHUNKS
    piece = span // nr
    lanes = rows // 128

    def remote(src, dst, sems, slot, **device):
        return pltpu.make_async_remote_copy(
            src_ref=src,
            dst_ref=dst,
            send_sem=sems.at[(0,) + slot],
            recv_sem=sems.at[(1,) + slot],
            device_id=device,
            device_id_type=MESH,
        )

    def next_shard(k):
        return lax.rem(shard + k, ns)

    def next_rep(k):
        return lax.rem(rep + k, nr)

    def next_chip(k):
        return lax.rem(chip + k, chips)

    barrier = pltpu.get_barrier_semaphore()
    for k in range(1, ns):
        pl.semaphore_signal(barrier, inc=1, device_id={"shard": next_shard(k)}, device_id_type=MESH)
    for k in range(1, nr):
        pl.semaphore_signal(barrier, inc=1, device_id={"rep": next_rep(k)}, device_id_type=MESH)

    load_tok = pltpu.make_async_copy(tok_hbm, tok_v, loc.at[0])
    load_tok.start()
    load_w = pltpu.make_async_copy(w_hbm, w_v, loc.at[1])
    load_w.start()
    mine = pl.ds(pl.multiple_of(shard * count, count), count)
    own_tok = []
    for c in range(CHUNKS):
        col = pl.multiple_of(shard * rows + c * span, 128)
        own_tok.append(
            pltpu.make_async_copy(
                tok_hbm.at[:, pl.ds(col, span)], tok_g.at[c, mine], loc.at[2 + c]
            )
        )
        own_tok[c].start()
    load_tok.wait()

    @pl.loop(0, count // 16)
    def _(step):
        row = pl.multiple_of(step * 16, 16)
        block = pl.ds(row, 16)
        square = jnp.zeros((16, 128), jnp.float32)
        for col in range(0, features, 128):
            wide = tok_v[block, col : col + 128].astype(jnp.float32)
            square = square + wide * wide
        mean = jnp.sum(square, axis=1, keepdims=True) * (1.0 / features)
        inv = lax.rsqrt(mean + eps_norm)
        inv_ref[block, :] = jnp.broadcast_to(inv, (16, 128))
        scaled = (cot_ref[block, :].astype(jnp.float32) * inv).astype(jnp.bfloat16)
        cot_g[pl.ds(pl.multiple_of(shard * count + row, 16), 16), :] = scaled

    pl.semaphore_wait(barrier, ns - 1 + nr - 1)

    cot_copies = [
        remote(cot_g.at[mine], cot_g.at[mine], cot_sem, (k - 1,), shard=next_shard(k))
        for k in range(1, ns)
    ]
    for copy in cot_copies:
        copy.start()
    tok_copies = []
    for c in range(CHUNKS):
        for k in range(1, ns):
            col = pl.multiple_of(next_shard(k) * rows + c * span, 128)
            tok_copies.append(
                remote(
                    tok_hbm.at[:, pl.ds(col, span)],
                    tok_g.at[c, mine],
                    tok_sem,
                    (c, k - 1),
                    shard=next_shard(k),
                )
            )
            tok_copies[-1].start()

    load_w.wait()
    for copy in cot_copies:
        copy.wait_recv()

    @pl.loop(0, CHUNKS)
    def _(c):
        rows_c = pl.ds(pl.multiple_of(c * span, 128), span)
        ng[c] = lax.dot_general(
            cot_g[...],
            w_v[rows_c, :],
            (((1,), (1,)), ((), ())),
            preferred_element_type=jnp.float32,
        ).astype(jnp.bfloat16)

    own_ng = pltpu.make_async_copy(ng.at[:, mine], ng_home.at[shard], loc.at[2 + CHUNKS])
    own_ng.start()
    ng_copies = []
    for k in range(1, ns):
        theirs = pl.ds(pl.multiple_of(next_shard(k) * count, count), count)
        ng_copies.append(
            remote(ng.at[:, theirs], ng_home.at[shard], ng_sem, (k - 1,), shard=next_shard(k))
        )

    core_copies = [
        remote(part.at[c, :, 1 - core], core_recv.at[c], core_sem, (c,), rep=partner)
        for c in range(CHUNKS)
    ]
    chip_copies = [
        [
            remote(
                red.at[c, next_chip(k)],
                chip_recv.at[c, k - 1],
                chip_sem,
                (c, k - 1),
                rep=next_chip(k) * 2 + core,
            )
            for k in range(1, chips)
        ]
        for c in range(CHUNKS)
    ]

    def out_rows(c, owner):
        return pl.ds(pl.multiple_of(c * span + owner * piece, 16), piece)

    ag_copies, fwd_copies, own_nw = [], [], []
    for c in range(CHUNKS):
        here = out_rows(c, rep)
        targets = [next_chip(k) * 2 + core for k in range(1, chips)] + [partner]
        ag_copies.append(
            [
                remote(nw_own.at[c], nw_hbm.at[here], ag_sem, (c, i), rep=target)
                for i, target in enumerate(targets)
            ]
        )
        own_nw.append(
            pltpu.make_async_copy(nw_own.at[c], nw_hbm.at[here], loc.at[3 + CHUNKS + c])
        )
        steps = []
        for k in range(1, chips):
            there = out_rows(c, next_chip(chips - k) * 2 + core)
            steps.append(
                remote(nw_hbm.at[there], nw_hbm.at[there], fwd_sem, (c, k - 1), rep=partner)
            )
        fwd_copies.append(steps)

    def form(c):
        own_tok[c].wait()
        for k in range(ns - 1):
            tok_copies[c * (ns - 1) + k].wait_recv()
        product = lax.dot_general(
            tok_g[c], cot_g[...], (((0,), (0,)), ((), ())), preferred_element_type=jnp.float32
        )
        for j in range(nr):
            part[c, j // 2, j % 2] = product[j * piece : (j + 1) * piece].astype(jnp.bfloat16)
        core_copies[c].start()

        def add(step, total):
            block = pl.ds(pl.multiple_of(step * 32, 32), 32)
            term = ng[c, block, :].astype(jnp.float32) * tok_g[c, block, :].astype(jnp.float32)
            return total + term

        total = lax.fori_loop(
            0, ns * count // 32, add, jnp.zeros((32, span), jnp.float32)
        )
        line = jnp.sum(total, axis=0, keepdims=True)
        for i in range(span // 128):
            k = c * (span // 128) + i
            gain_own[k : k + 1, :] = line[:, i * 128 : (i + 1) * 128]

    def reduce_core(c):
        core_copies[c].wait_recv()
        for q in range(chips):
            both = part[c, q, core].astype(jnp.float32) + core_recv[c, q].astype(jnp.float32)
            red[c, q] = both.astype(jnp.bfloat16)
        for copy in chip_copies[c]:
            copy.start()

    def update(c):
        for copy in chip_copies[c]:
            copy.wait_recv()
        tops = [jnp.zeros((1, 128), jnp.float32)] * 2
        for row in range(0, piece, 16):
            block = slice(row, row + 16)
            grad = red[c, chip, block, :].astype(jnp.float32)
            for k in range(chips - 1):
                grad = grad + chip_recv[c, k, block, :].astype(jnp.float32)
            grad = grad * gain_rows[c, block, 0:1]
            weight = w_v[pl.ds(pl.multiple_of(c * span + rep * piece + row, 16), 16), :]
            new_part, first, second = adam_update(
                weight, grad, old_m[c, block, :], old_v[c, block, :]
            )
            nw_own[c, block, :] = new_part
            place = (
                lax.broadcasted_iota(jnp.int32, (16, 128), 0)
                + row
                - 2 * lax.broadcasted_iota(jnp.int32, (16, 128), 1)
            )
            hit = (place == 0) | (place == 1)
            for i, value in enumerate((jnp.abs(first), second)):
                top = jnp.max(value, axis=1, keepdims=True)
                spread = jnp.where(hit, jnp.broadcast_to(top, (16, 128)), 0.0)
                tops[i] = jnp.maximum(tops[i], jnp.max(spread, axis=0, keepdims=True))
        for copy in ag_copies[c]:
            copy.start()
        own_nw[c].start()
        for i in range(2):
            scale_own[2 * c + i : 2 * c + i + 1, :] = tops[i]

    def forward(c):
        for k in range(chips - 1):
            ag_copies[c][k].wait_recv()
            fwd_copies[c][k].start()

    scale_own[...] = jnp.zeros_like(scale_own)
    gain_own[...] = jnp.zeros_like(gain_own)
    form(0)
    reduce_core(0)
    form(1)
    reduce_core(1)
    for copy in ng_copies:
        copy.start()
    update(0)
    form(2)
    gain_copies = [
        remote(gain_own, gain_recv.at[k - 1], gain_sem, (k - 1,), rep=next_rep(k))
        for k in range(1, nr)
    ]
    reduce_core(2)
    for copy in gain_copies:
        copy.start()
    update(1)
    forward(0)
    update(2)
    scale_copies = [
        remote(scale_own, scale_recv.at[rep], scale_sem, (k - 1,), rep=next_rep(k))
        for k in range(1, nr)
    ]
    for copy in scale_copies:
        copy.start()
    scale_recv[rep] = scale_own[...]
    forward(1)
    total = gain_own[...]
    for k in range(nr - 1):
        gain_copies[k].wait_recv()
        total = total + gain_recv[k]
    gain_sum[...] = total
    gz_copies = [
        remote(gain_sum, gain_z.at[shard], gz_sem, (k - 1,), shard=next_shard(k))
        for k in range(1, ns)
    ]
    for copy in gz_copies:
        copy.start()
    gain_z[shard] = total
    forward(2)

    own_ng.wait()
    for copy in ng_copies:
        copy.wait_recv()

    @pl.loop(0, count // 16)
    def _(step):
        block = pl.ds(pl.multiple_of(step * 16, 16), 16)
        inner = jnp.zeros((16, 128), jnp.float32)
        for col in range(0, features, 128):
            p, c, o = col // rows, col % rows // span, col % span
            scaled = ng_home[p, c, block, o : o + 128].astype(jnp.float32) * gain_ref[:, col : col + 128]
            inner = inner + scaled * tok_v[block, col : col + 128].astype(jnp.float32)
        inv = inv_ref[block, 0:1]
        mean = jnp.sum(inner, axis=1, keepdims=True) * (1.0 / features)
        factor = jnp.broadcast_to(inv * inv * mean, (16, 128))
        for col in range(0, features, 128):
            p, c, o = col // rows, col % rows // span, col % span
            scaled = ng_home[p, c, block, o : o + 128].astype(jnp.float32) * gain_ref[:, col : col + 128]
            wide = tok_v[block, col : col + 128].astype(jnp.float32)
            ig_ref[block, col : col + 128] = (scaled - wide * factor).astype(jnp.bfloat16)

    for copy in gz_copies + scale_copies:
        copy.wait_recv()
    gain_out[...] = gain_z[...]
    scale_out[...] = scale_recv[...]
    for c in range(CHUNKS):
        own_nw[c].wait()
        ag_copies[c][chips - 1].wait_recv()
        for copy in fwd_copies[c]:
            copy.wait_recv()
            copy.wait_send()
        for copy in ag_copies[c] + chip_copies[c]:
            copy.wait_send()
        core_copies[c].wait_send()
    for copy in cot_copies + tok_copies + ng_copies + gain_copies + scale_copies + gz_copies:
        copy.wait_send()


def decode_rows(codes_m, codes_v, scale_m, scale_v, qmap_m, qmap_v, part, row_group):
    width = codes_m.shape[1]
    rows = CHUNKS * part

    def spread(scale):
        mine = scale.reshape(CHUNKS, -1, part // row_group)
        mine = lax.dynamic_index_in_dim(mine, lax.axis_index("rep"), 1, keepdims=False)
        return jnp.broadcast_to(jnp.repeat(mine.reshape(-1), row_group)[:, None], (rows, 128))

    vmem = pl.BlockSpec(memory_space=pltpu.VMEM)
    anywhere = pl.BlockSpec(memory_space=pl.ANY)
    shape = jax.ShapeDtypeStruct((rows, width), jnp.float32)
    chunk_rows = codes_m.shape[0] // CHUNKS
    return pl.pallas_call(
        lambda *refs: decode_kernel(CHUNKS, chunk_rows, part, *refs),
        out_shape=(shape, shape),
        in_specs=[vmem] * 4 + [anywhere] * 2,
        out_specs=(vmem, vmem),
        scratch_shapes=[
            pltpu.VMEM((rows, width), jnp.int32),
            pltpu.VMEM((rows, width), jnp.int32),
            pltpu.SemaphoreType.DMA((2, CHUNKS)),
        ],
        compiler_params=pltpu.CompilerParams(vmem_limit_bytes=16 * 2**20),
        name="decode",
    )(qmap_m.reshape(2, 128), qmap_v.reshape(2, 128), spread(scale_m), spread(scale_v), codes_m, codes_v)


def fused_shards(
    tokens, key_cot, norm_gain, key_weight, codes_m, codes_v, scale_m, scale_v, qmap_m, qmap_v
):
    count, features = tokens.shape
    rows, width = key_weight.shape
    row_group = BLOCK // width
    nr, ns = lax.axis_size("rep"), lax.axis_size("shard")
    rep, shard = lax.axis_index("rep"), lax.axis_index("shard")
    span = rows // CHUNKS
    part = span // nr
    chips = nr // 2
    old_m, old_v = decode_rows(codes_m, codes_v, scale_m, scale_v, qmap_m, qmap_v, part, row_group)
    gains = lax.dynamic_index_in_dim(norm_gain.reshape(ns, CHUNKS, nr, part), shard, 0, False)
    gains = lax.dynamic_index_in_dim(gains, rep, 1, False)
    gain_rows = jnp.broadcast_to(gains[:, :, None], (CHUNKS, part, 128))
    vmem = pl.BlockSpec(memory_space=pltpu.VMEM)
    anywhere = pl.BlockSpec(memory_space=pl.ANY)
    lanes = -(-rows // 1024) * 8
    levels = -(-2 * CHUNKS // 8) * 8
    half, full = jnp.bfloat16, jnp.float32
    dma = pltpu.SemaphoreType.DMA
    input_grad, new_weight, gain_tiles, scale_tiles = pl.pallas_call(
        lambda *refs: fused_kernel(nr, ns, *refs),
        out_shape=(
            jax.ShapeDtypeStruct((count, features), half),
            jax.ShapeDtypeStruct((rows, width), half),
            jax.ShapeDtypeStruct((ns, lanes, 128), full),
            jax.ShapeDtypeStruct((nr, levels, 128), full),
        ),
        in_specs=[anywhere, vmem, vmem, vmem, anywhere, vmem, vmem],
        out_specs=(vmem, anywhere, vmem, vmem),
        scratch_shapes=[
            pltpu.VMEM((count, features), half),
            pltpu.VMEM((rows, width), half),
            pltpu.VMEM((CHUNKS, ns * count, span), half),
            pltpu.VMEM((ns * count, width), half),
            pltpu.VMEM((CHUNKS, ns * count, span), half),
            pltpu.VMEM((ns, CHUNKS, count, span), half),
            pltpu.VMEM((CHUNKS, chips, 2, part, width), half),
            pltpu.VMEM((CHUNKS, chips, part, width), half),
            pltpu.VMEM((CHUNKS, chips, part, width), half),
            pltpu.VMEM((CHUNKS, chips - 1, part, width), half),
            pltpu.VMEM((CHUNKS, part, width), half),
            pltpu.VMEM((count, 128), full),
            pltpu.VMEM((lanes, 128), full),
            pltpu.VMEM((nr - 1, lanes, 128), full),
            pltpu.VMEM((lanes, 128), full),
            pltpu.VMEM((ns, lanes, 128), full),
            pltpu.VMEM((levels, 128), full),
            pltpu.VMEM((nr, levels, 128), full),
            dma((3 + 2 * CHUNKS,)),
            dma((2, ns - 1)),
            dma((2, CHUNKS, ns - 1)),
            dma((2, ns - 1)),
            dma((2, CHUNKS)),
            dma((2, CHUNKS, chips - 1)),
            dma((2, CHUNKS, chips)),
            dma((2, CHUNKS, chips - 1)),
            dma((2, nr - 1)),
            dma((2, ns - 1)),
            dma((2, nr - 1)),
        ],
        compiler_params=pltpu.CompilerParams(
            collective_id=0, has_side_effects=True, vmem_limit_bytes=48 * 2**20
        ),
        cost_estimate=pl.CostEstimate(
            flops=4 * ns * count * rows * width, bytes_accessed=12 * 2**20, transcendentals=0
        ),
        name="fused",
    )(
        tokens,
        key_cot,
        norm_gain.reshape(1, features),
        gain_rows,
        key_weight,
        old_m.reshape(CHUNKS, part, width),
        old_v.reshape(CHUNKS, part, width),
    )
    gain_grad = gain_tiles[:, : rows // 128].reshape(features)
    maxima = scale_tiles[:, : 2 * CHUNKS, : part // row_group]
    maxima = maxima.reshape(nr, CHUNKS, 2, part // row_group).transpose(2, 1, 0, 3).reshape(2, -1)
    return (input_grad, gain_grad, new_weight, maxima[0], maxima[1])


def shards(tokens, key_cot, norm_gain, key_weight, *rest):
    part = key_weight.shape[0] // CHUNKS // lax.axis_size("rep")
    even = (
        key_weight.shape[0] % (CHUNKS * 128) == 0
        and part % 16 == 0
        and lax.axis_size("rep") % 2 == 0
        and key_cot.shape[1] * 2 == BLOCK
    )
    body = fused_shards if even else plain_shards
    return body(tokens, key_cot, norm_gain, key_weight, *rest)


def solution(mesh):
    placed = (
        P(("rep", "shard"), None),
        P(("rep", "shard"), None),
        P(),
        P("shard", None),
        P("shard", None),
        P("shard", None),
        P("shard"),
        P("shard"),
        P(),
        P(),
    )
    return jax.shard_map(
        shards,
        mesh=mesh,
        in_specs=placed,
        out_specs=(P(("rep", "shard"), None), P(), P("shard", None), P("shard"), P("shard")),
        check_vma=False,
    )
```

```python
import math

import jax
import jax.numpy as jnp
from jax import lax
from jax.experimental import pallas as pl
from jax.experimental.pallas import tpu as pltpu
from jax.sharding import PartitionSpec as P

BLOCK = 2048
CHUNKS = 3
MESH = pl.DeviceIdType.MESH


eps_norm = 1e-06
beta_one = 0.9
beta_two = 0.95
adam_eps = 1e-08
learn_rate = 0.01
decay_rate = 0.1
bias_one = 1.0 - 0.9**10
bias_two = 1.0 - 0.95**10


def normalize(tokens, norm_gain):
    wide = tokens.astype(jnp.float32)
    inv_rms = lax.rsqrt(jnp.mean(wide * wide, axis=-1, keepdims=True) + eps_norm)
    normed = (wide * inv_rms * norm_gain).astype(jnp.bfloat16)
    return (wide, inv_rms, normed)


def norm_backward(wide, inv_rms, norm_gain, normed_grad):
    scaled = normed_grad * norm_gain
    inner = jnp.mean(scaled * wide, axis=-1, keepdims=True)
    input_grad = (inv_rms * scaled - wide * inv_rms**3 * inner).astype(jnp.bfloat16)
    gain_term = jnp.sum(normed_grad * wide * inv_rms, axis=0)
    return (input_grad, gain_term)


def rounded(value):
    lowered = lax.optimization_barrier(value.astype(jnp.bfloat16))
    return lowered.astype(jnp.float32)


def decode(codes, table):
    high_part = codes // 16
    low_part = codes - high_part * 16
    levels = lax.broadcasted_iota(jnp.int32, (16, 1, 1), 0)
    pick_low = (low_part[None] == levels).astype(jnp.float32)
    pick_high = (high_part[None] == levels).astype(jnp.float32)
    table_grid = table.reshape(16, 16)
    by_high = jnp.einsum("hl,lrk->hrk", table_grid, pick_low, precision=lax.Precision.HIGHEST)
    return jnp.sum(pick_high * by_high, axis=0)


def adam_update(weight, grad, old_m, old_v):
    first = beta_one * old_m + (1.0 - beta_one) * grad
    second = beta_two * old_v + (1.0 - beta_two) * grad * grad
    direction = first / bias_one / (jnp.sqrt(second / bias_two) + adam_eps)
    new_weight = (
        weight.astype(jnp.float32) * (1.0 - learn_rate * decay_rate) - learn_rate * direction
    ).astype(jnp.bfloat16)
    return (new_weight, first, second)


def block_max(values, row_group):
    blocks = values.reshape(values.shape[0] // row_group, -1)
    return jnp.max(jnp.abs(blocks), axis=1)


def optimize(
    weight, grad, codes_first, codes_second, scales_first, scales_second, qmap_m, qmap_v, row_group
):
    rows, width = weight.shape
    span_rows = math.gcd(rows, 64)
    span_count = rows // span_rows
    per_span = span_rows // row_group

    def one_span(pieces):
        weight_part, grad_part, code_one, code_two, scale_one, scale_two = pieces
        old_m = (
            decode(code_one, qmap_m).reshape(per_span, row_group, width) * scale_one[:, None, None]
        ).reshape(span_rows, width)
        old_v = (
            decode(code_two, qmap_v).reshape(per_span, row_group, width) * scale_two[:, None, None]
        ).reshape(span_rows, width)
        new_part, first, second = adam_update(weight_part, grad_part, old_m, old_v)
        return (new_part, block_max(first, row_group), block_max(second, row_group))

    pieces = (
        weight.reshape(span_count, span_rows, width),
        grad.reshape(span_count, span_rows, width),
        codes_first.reshape(span_count, span_rows, width),
        codes_second.reshape(span_count, span_rows, width),
        scales_first.reshape(span_count, per_span),
        scales_second.reshape(span_count, per_span),
    )
    new_weight, new_first, new_second = lax.map(one_span, pieces)
    return (new_weight.reshape(rows, width), new_first.reshape(-1), new_second.reshape(-1))


def plain_shards(
    tokens, key_cot, norm_gain, key_weight, codes_m, codes_v, scale_m, scale_v, qmap_m, qmap_v
):
    width = key_cot.shape[1]
    row_group = BLOCK // width
    wide, inv_rms, normed = normalize(tokens, norm_gain)
    group_cot = lax.all_gather(key_cot, "shard", axis=0, tiled=True)
    local_cols = jnp.einsum("tk,dk->td", group_cot, key_weight, preferred_element_type=jnp.float32)
    normed_grad = lax.all_to_all(local_cols, "shard", split_axis=0, concat_axis=1, tiled=True)
    input_grad, gain_term = norm_backward(wide, inv_rms, norm_gain, normed_grad)
    gain_grad = lax.psum(gain_term, ("rep", "shard"))
    shard_count = lax.axis_size("shard")
    rep_count = lax.axis_size("rep")
    slice_rows = key_weight.shape[0] // rep_count
    reordered = normed.reshape(normed.shape[0], shard_count, rep_count, slice_rows)
    reordered = reordered.transpose(0, 2, 1, 3).reshape(normed.shape)
    grad = lax.psum_scatter(
        rounded(jnp.einsum("td,tk->dk", reordered, key_cot, preferred_element_type=jnp.float32)),
        ("rep", "shard"),
        scatter_dimension=0,
        tiled=True,
    )
    first_row = lax.axis_index("rep") * slice_rows
    first_block = lax.axis_index("rep") * (slice_rows // row_group)

    def take_rows(array_in):
        return lax.dynamic_slice_in_dim(array_in, first_row, slice_rows, 0)

    def take_blocks(array_in):
        return lax.dynamic_slice_in_dim(array_in, first_block, slice_rows // row_group, 0)

    part_weight, part_m, part_v = optimize(
        take_rows(key_weight),
        grad,
        take_rows(codes_m),
        take_rows(codes_v),
        take_blocks(scale_m),
        take_blocks(scale_v),
        qmap_m,
        qmap_v,
        row_group,
    )
    new_weight = lax.all_gather(part_weight, "rep", axis=0, tiled=True)
    new_scale_m, new_scale_v = (
        lax.all_gather(part_m, "rep", axis=0, tiled=True),
        lax.all_gather(part_v, "rep", axis=0, tiled=True),
    )
    return (input_grad, gain_grad, new_weight, new_scale_m, new_scale_v)


def lookup(codes, table):
    low = codes & 127
    first = jnp.take_along_axis(table[0], low, axis=1)
    second = jnp.take_along_axis(table[1], low, axis=1)
    return jnp.where(codes >= 128, second, first)


def column(values, first, repeat, count):
    row = lax.broadcasted_iota(jnp.int32, (count, 128), 0)
    out = jnp.full((count, 128), values[first], jnp.float32)
    for i in range(1, count // repeat):
        out = jnp.where(row >= i * repeat, values[first + i], out)
    return out


def fused_kernel(
    nr,
    ns,
    tok_hbm,
    cot_ref,
    gain_ref,
    gains,
    w_hbm,
    codes_m,
    codes_v,
    scale_m,
    scale_v,
    table_m,
    table_v,
    ig_ref,
    nw_hbm,
    gain_out,
    scale_out,
    tok_v,
    w_v,
    tok_g,
    cot_g,
    ng,
    ng_home,
    part,
    core_recv,
    red,
    chip_recv,
    nw_own,
    inv_ref,
    gain_own,
    gain_recv,
    gain_sum,
    gain_z,
    scale_own,
    scale_recv,
    held_codes,
    old,
    code_sem,
    loc,
    cot_sem,
    tok_sem,
    ng_sem,
    core_sem,
    chip_sem,
    ag_sem,
    fwd_sem,
    gain_sem,
    gz_sem,
    scale_sem,
):
    rep, shard = lax.axis_index("rep"), lax.axis_index("shard")
    chips = nr // 2
    chip, core = rep // 2, rep % 2
    partner = rep + 1 - 2 * core
    count, features = tok_v.shape
    rows, width = w_v.shape
    span = rows // CHUNKS
    piece = span // nr
    lanes = rows // 128

    def remote(src, dst, sems, slot, **device):
        return pltpu.make_async_remote_copy(
            src_ref=src,
            dst_ref=dst,
            send_sem=sems.at[(0,) + slot],
            recv_sem=sems.at[(1,) + slot],
            device_id=device,
            device_id_type=MESH,
        )

    def next_shard(k):
        return lax.rem(shard + k, ns)

    def next_rep(k):
        return lax.rem(rep + k, nr)

    def next_chip(k):
        return lax.rem(chip + k, chips)

    barrier = pltpu.get_barrier_semaphore()
    for k in range(1, ns):
        pl.semaphore_signal(barrier, inc=1, device_id={"shard": next_shard(k)}, device_id_type=MESH)
    for k in range(1, nr):
        pl.semaphore_signal(barrier, inc=1, device_id={"rep": next_rep(k)}, device_id_type=MESH)

    load_tok = pltpu.make_async_copy(tok_hbm, tok_v, loc.at[0])
    load_tok.start()
    load_w = pltpu.make_async_copy(w_hbm, w_v, loc.at[1])
    load_w.start()
    loads = []
    for i, codes in enumerate((codes_m, codes_v)):
        for c in range(CHUNKS):
            start = pl.multiple_of(c * span + rep * piece, 16)
            loads.append(
                pltpu.make_async_copy(
                    codes.at[pl.ds(start, piece)], held_codes.at[i, c], code_sem.at[i, c]
                )
            )
            loads[-1].start()
    mine = pl.ds(pl.multiple_of(shard * count, count), count)
    own_tok = []
    for c in range(CHUNKS):
        col = pl.multiple_of(shard * rows + c * span, 128)
        own_tok.append(
            pltpu.make_async_copy(
                tok_hbm.at[:, pl.ds(col, span)], tok_g.at[c, mine], loc.at[2 + c]
            )
        )
        own_tok[c].start()
    load_tok.wait()

    @pl.loop(0, count // 16)
    def _(step):
        row = pl.multiple_of(step * 16, 16)
        block = pl.ds(row, 16)
        square = jnp.zeros((16, 128), jnp.float32)
        for col in range(0, features, 128):
            wide = tok_v[block, col : col + 128].astype(jnp.float32)
            square = square + wide * wide
        mean = jnp.sum(square, axis=1, keepdims=True) * (1.0 / features)
        inv = lax.rsqrt(mean + eps_norm)
        inv_ref[block, :] = jnp.broadcast_to(inv, (16, 128))
        scaled = (cot_ref[block, :].astype(jnp.float32) * inv).astype(jnp.bfloat16)
        cot_g[pl.ds(pl.multiple_of(shard * count + row, 16), 16), :] = scaled

    pl.semaphore_wait(barrier, ns - 1 + nr - 1)

    tok_copies = []
    for c in range(CHUNKS):
        for k in range(1, ns):
            col = pl.multiple_of(next_shard(k) * rows + c * span, 128)
            tok_copies.append(
                remote(
                    tok_hbm.at[:, pl.ds(col, span)],
                    tok_g.at[c, mine],
                    tok_sem,
                    (c, k - 1),
                    shard=next_shard(k),
                )
            )

    def send_tokens(c):
        for k in range(ns - 1):
            tok_copies[c * (ns - 1) + k].start()

    def decode(i):
        table_ref, scale = ((table_m, scale_m), (table_v, scale_v))[i]
        tables = [jnp.broadcast_to(table_ref[k : k + 1, :], (8, 128)) for k in range(2)]
        group = BLOCK // width
        for c in range(CHUNKS):
            loads[i * CHUNKS + c].wait()

            @pl.loop(0, piece // 8)
            def _(step):
                block = pl.ds(pl.multiple_of(step * 8, 8), 8)
                first = (c * span + rep * piece) // group + step * (8 // group)
                factor = column(scale, first, group, 8)
                for col in range(0, width, 128):
                    value = lookup(held_codes[i, c, block, col : col + 128], tables)
                    old[i, c, block, col : col + 128] = value * factor

    def relay(way, t):
        origin = jnp.clip(shard - way * t, 0, ns - 1)
        block = cot_g.at[pl.ds(pl.multiple_of(origin * count, count), count)]
        there = jnp.clip(shard + way, 0, ns - 1)
        return remote(block, block, cot_sem, ((1 - way) // 2, t), shard=there)

    def sends(way, t):
        if way > 0:
            return (shard + 1 < ns) & (shard >= t)
        return (shard >= 1) & (shard + t < ns)

    def takes(way, t):
        return shard >= t + 1 if way > 0 else shard + t + 1 < ns

    for t in range(ns - 1):
        for way in (1, -1):
            if t > 0:

                @pl.when(takes(way, t - 1))
                def _():
                    relay(way, t - 1).wait_recv()

            @pl.when(sends(way, t))
            def _():
                relay(way, t).start()

        if t == 0:
            decode(0)
        elif t == 1:
            send_tokens(0)
            decode(1)
    if ns < 3:
        send_tokens(0)
        decode(1)
    for c in range(1, CHUNKS):
        send_tokens(c)
    for way in (1, -1):

        @pl.when(takes(way, ns - 2))
        def _():
            relay(way, ns - 2).wait_recv()

    load_w.wait()
    @pl.loop(0, CHUNKS)
    def _(c):
        rows_c = pl.ds(pl.multiple_of(c * span, 128), span)
        ng[c] = lax.dot_general(
            cot_g[...],
            w_v[rows_c, :],
            (((1,), (1,)), ((), ())),
            preferred_element_type=jnp.float32,
        ).astype(jnp.bfloat16)

    own_ng = pltpu.make_async_copy(ng.at[:, mine], ng_home.at[shard], loc.at[2 + CHUNKS])
    own_ng.start()
    ng_copies = []
    for k in range(1, ns):
        theirs = pl.ds(pl.multiple_of(next_shard(k) * count, count), count)
        ng_copies.append(
            remote(ng.at[:, theirs], ng_home.at[shard], ng_sem, (k - 1,), shard=next_shard(k))
        )

    core_copies = [
        remote(part.at[c, :, 1 - core], core_recv.at[c], core_sem, (c,), rep=partner)
        for c in range(CHUNKS)
    ]
    chip_copies = [
        [
            remote(
                red.at[c, next_chip(k)],
                chip_recv.at[c, k - 1],
                chip_sem,
                (c, k - 1),
                rep=next_chip(k) * 2 + core,
            )
            for k in range(1, chips)
        ]
        for c in range(CHUNKS)
    ]

    def out_rows(c, owner):
        return pl.ds(pl.multiple_of(c * span + owner * piece, 16), piece)

    ag_copies, fwd_copies, own_nw = [], [], []
    for c in range(CHUNKS):
        here = out_rows(c, rep)
        targets = [next_chip(k) * 2 + core for k in range(1, chips)] + [partner]
        ag_copies.append(
            [
                remote(nw_own.at[c], nw_hbm.at[here], ag_sem, (c, i), rep=target)
                for i, target in enumerate(targets)
            ]
        )
        own_nw.append(
            pltpu.make_async_copy(nw_own.at[c], nw_hbm.at[here], loc.at[3 + CHUNKS + c])
        )
        steps = []
        for k in range(1, chips):
            there = out_rows(c, next_chip(chips - k) * 2 + core)
            steps.append(
                remote(nw_hbm.at[there], nw_hbm.at[there], fwd_sem, (c, k - 1), rep=partner)
            )
        fwd_copies.append(steps)

    def form(c):
        own_tok[c].wait()
        for k in range(ns - 1):
            tok_copies[c * (ns - 1) + k].wait_recv()
        product = lax.dot_general(
            tok_g[c], cot_g[...], (((0,), (0,)), ((), ())), preferred_element_type=jnp.float32
        )
        for j in range(nr):
            part[c, j // 2, j % 2] = product[j * piece : (j + 1) * piece].astype(jnp.bfloat16)
        core_copies[c].start()

        def add(step, total):
            block = pl.ds(pl.multiple_of(step * 32, 32), 32)
            term = ng[c, block, :].astype(jnp.float32) * tok_g[c, block, :].astype(jnp.float32)
            return total + term

        total = lax.fori_loop(
            0, ns * count // 32, add, jnp.zeros((32, span), jnp.float32)
        )
        line = jnp.sum(total, axis=0, keepdims=True)
        for i in range(span // 128):
            k = c * (span // 128) + i
            gain_own[k : k + 1, :] = line[:, i * 128 : (i + 1) * 128]

    def reduce_core(c):
        core_copies[c].wait_recv()
        for q in range(chips):
            both = part[c, q, core].astype(jnp.float32) + core_recv[c, q].astype(jnp.float32)
            red[c, q] = both.astype(jnp.bfloat16)
        for copy in chip_copies[c]:
            copy.start()

    def update(c):
        for copy in chip_copies[c]:
            copy.wait_recv()
        tops = [jnp.zeros((1, 128), jnp.float32)] * 2
        for row in range(0, piece, 16):
            block = slice(row, row + 16)
            grad = red[c, chip, block, :].astype(jnp.float32)
            for k in range(chips - 1):
                grad = grad + chip_recv[c, k, block, :].astype(jnp.float32)
            first_gain = shard * rows + c * span + rep * piece + row
            grad = grad * column(gains, first_gain, 1, 16)[:, 0:1]
            weight = w_v[pl.ds(pl.multiple_of(c * span + rep * piece + row, 16), 16), :]
            new_part, first, second = adam_update(
                weight, grad, old[0, c, block, :], old[1, c, block, :]
            )
            nw_own[c, block, :] = new_part
            place = (
                lax.broadcasted_iota(jnp.int32, (16, 128), 0)
                + row
                - 2 * lax.broadcasted_iota(jnp.int32, (16, 128), 1)
            )
            hit = (place == 0) | (place == 1)
            for i, value in enumerate((jnp.abs(first), second)):
                top = jnp.max(value, axis=1, keepdims=True)
                spread = jnp.where(hit, jnp.broadcast_to(top, (16, 128)), 0.0)
                tops[i] = jnp.maximum(tops[i], jnp.max(spread, axis=0, keepdims=True))
        for copy in ag_copies[c]:
            copy.start()
        own_nw[c].start()
        for i in range(2):
            scale_own[2 * c + i : 2 * c + i + 1, :] = tops[i]

    def forward(c):
        for k in range(chips - 1):
            ag_copies[c][k].wait_recv()
            fwd_copies[c][k].start()

    scale_own[...] = jnp.zeros_like(scale_own)
    gain_own[...] = jnp.zeros_like(gain_own)
    form(0)
    reduce_core(0)
    form(1)
    reduce_core(1)
    for copy in ng_copies:
        copy.start()
    update(0)
    form(2)
    gain_copies = [
        remote(gain_own, gain_recv.at[k - 1], gain_sem, (k - 1,), rep=next_rep(k))
        for k in range(1, nr)
    ]
    reduce_core(2)
    for copy in gain_copies:
        copy.start()
    update(1)
    forward(0)
    update(2)
    scale_copies = [
        remote(scale_own, scale_recv.at[rep], scale_sem, (k - 1,), rep=next_rep(k))
        for k in range(1, nr)
    ]
    for copy in scale_copies:
        copy.start()
    scale_recv[rep] = scale_own[...]
    forward(1)
    total = gain_own[...]
    for k in range(nr - 1):
        gain_copies[k].wait_recv()
        total = total + gain_recv[k]
    gain_sum[...] = total
    gz_copies = [
        remote(gain_sum, gain_z.at[shard], gz_sem, (k - 1,), shard=next_shard(k))
        for k in range(1, ns)
    ]
    for copy in gz_copies:
        copy.start()
    gain_z[shard] = total
    forward(2)

    own_ng.wait()
    for copy in ng_copies:
        copy.wait_recv()

    @pl.loop(0, count // 16)
    def _(step):
        block = pl.ds(pl.multiple_of(step * 16, 16), 16)
        inner = jnp.zeros((16, 128), jnp.float32)
        for col in range(0, features, 128):
            p, c, o = col // rows, col % rows // span, col % span
            scaled = ng_home[p, c, block, o : o + 128].astype(jnp.float32) * gain_ref[:, col : col + 128]
            inner = inner + scaled * tok_v[block, col : col + 128].astype(jnp.float32)
        inv = inv_ref[block, 0:1]
        mean = jnp.sum(inner, axis=1, keepdims=True) * (1.0 / features)
        factor = jnp.broadcast_to(inv * inv * mean, (16, 128))
        for col in range(0, features, 128):
            p, c, o = col // rows, col % rows // span, col % span
            scaled = ng_home[p, c, block, o : o + 128].astype(jnp.float32) * gain_ref[:, col : col + 128]
            wide = tok_v[block, col : col + 128].astype(jnp.float32)
            ig_ref[block, col : col + 128] = (scaled - wide * factor).astype(jnp.bfloat16)

    for copy in gz_copies + scale_copies:
        copy.wait_recv()
    gain_out[...] = gain_z[...]
    scale_out[...] = scale_recv[...]
    for c in range(CHUNKS):
        own_nw[c].wait()
        ag_copies[c][chips - 1].wait_recv()
        for copy in fwd_copies[c]:
            copy.wait_recv()
            copy.wait_send()
        for copy in ag_copies[c] + chip_copies[c]:
            copy.wait_send()
        core_copies[c].wait_send()
    for t in range(ns - 1):
        for way in (1, -1):

            @pl.when(sends(way, t))
            def _():
                relay(way, t).wait_send()

    for copy in tok_copies + ng_copies + gain_copies + scale_copies + gz_copies:
        copy.wait_send()


def fused_shards(
    tokens, key_cot, norm_gain, key_weight, codes_m, codes_v, scale_m, scale_v, qmap_m, qmap_v
):
    count, features = tokens.shape
    rows, width = key_weight.shape
    row_group = BLOCK // width
    nr, ns = lax.axis_size("rep"), lax.axis_size("shard")
    span = rows // CHUNKS
    part = span // nr
    chips = nr // 2
    vmem = pl.BlockSpec(memory_space=pltpu.VMEM)
    anywhere = pl.BlockSpec(memory_space=pl.ANY)
    smem = pl.BlockSpec(memory_space=pltpu.SMEM)
    lanes = -(-rows // 1024) * 8
    levels = -(-2 * CHUNKS // 8) * 8
    half, full = jnp.bfloat16, jnp.float32
    dma = pltpu.SemaphoreType.DMA
    input_grad, new_weight, gain_tiles, scale_tiles = pl.pallas_call(
        lambda *refs: fused_kernel(nr, ns, *refs),
        out_shape=(
            jax.ShapeDtypeStruct((count, features), half),
            jax.ShapeDtypeStruct((rows, width), half),
            jax.ShapeDtypeStruct((ns, lanes, 128), full),
            jax.ShapeDtypeStruct((nr, levels, 128), full),
        ),
        in_specs=[anywhere, vmem, vmem, smem] + [anywhere] * 3 + [smem] * 2 + [vmem] * 2,
        out_specs=(vmem, anywhere, vmem, vmem),
        scratch_shapes=[
            pltpu.VMEM((count, features), half),
            pltpu.VMEM((rows, width), half),
            pltpu.VMEM((CHUNKS, ns * count, span), half),
            pltpu.VMEM((ns * count, width), half),
            pltpu.VMEM((CHUNKS, ns * count, span), half),
            pltpu.VMEM((ns, CHUNKS, count, span), half),
            pltpu.VMEM((CHUNKS, chips, 2, part, width), half),
            pltpu.VMEM((CHUNKS, chips, part, width), half),
            pltpu.VMEM((CHUNKS, chips, part, width), half),
            pltpu.VMEM((CHUNKS, chips - 1, part, width), half),
            pltpu.VMEM((CHUNKS, part, width), half),
            pltpu.VMEM((count, 128), full),
            pltpu.VMEM((lanes, 128), full),
            pltpu.VMEM((nr - 1, lanes, 128), full),
            pltpu.VMEM((lanes, 128), full),
            pltpu.VMEM((ns, lanes, 128), full),
            pltpu.VMEM((levels, 128), full),
            pltpu.VMEM((nr, levels, 128), full),
            pltpu.VMEM((2, CHUNKS, part, width), jnp.int32),
            pltpu.VMEM((2, CHUNKS, part, width), full),
            dma((2, CHUNKS)),
            dma((3 + 2 * CHUNKS,)),
            dma((2, 2, ns - 1)),
            dma((2, CHUNKS, ns - 1)),
            dma((2, ns - 1)),
            dma((2, CHUNKS)),
            dma((2, CHUNKS, chips - 1)),
            dma((2, CHUNKS, chips)),
            dma((2, CHUNKS, chips - 1)),
            dma((2, nr - 1)),
            dma((2, ns - 1)),
            dma((2, nr - 1)),
        ],
        compiler_params=pltpu.CompilerParams(
            collective_id=0, has_side_effects=True, vmem_limit_bytes=48 * 2**20
        ),
        cost_estimate=pl.CostEstimate(
            flops=4 * ns * count * rows * width, bytes_accessed=12 * 2**20, transcendentals=0
        ),
        name="fused",
    )(
        tokens,
        key_cot,
        norm_gain.reshape(1, features),
        norm_gain,
        key_weight,
        codes_m,
        codes_v,
        scale_m,
        scale_v,
        qmap_m.reshape(2, 128),
        qmap_v.reshape(2, 128),
    )
    gain_grad = gain_tiles[:, : rows // 128].reshape(features)
    maxima = scale_tiles[:, : 2 * CHUNKS, : part // row_group]
    maxima = maxima.reshape(nr, CHUNKS, 2, part // row_group).transpose(2, 1, 0, 3).reshape(2, -1)
    return (input_grad, gain_grad, new_weight, maxima[0], maxima[1])


def shards(tokens, key_cot, norm_gain, key_weight, *rest):
    part = key_weight.shape[0] // CHUNKS // lax.axis_size("rep")
    even = (
        key_weight.shape[0] % (CHUNKS * 128) == 0
        and part % 16 == 0
        and lax.axis_size("rep") % 2 == 0
        and key_cot.shape[1] * 2 == BLOCK
    )
    body = fused_shards if even else plain_shards
    return body(tokens, key_cot, norm_gain, key_weight, *rest)


def solution(mesh):
    placed = (
        P(("rep", "shard"), None),
        P(("rep", "shard"), None),
        P(),
        P("shard", None),
        P("shard", None),
        P("shard", None),
        P("shard"),
        P("shard"),
        P(),
        P(),
    )
    return jax.shard_map(
        shards,
        mesh=mesh,
        in_specs=placed,
        out_specs=(P(("rep", "shard"), None), P(), P("shard", None), P("shard"), P("shard")),
        check_vma=False,
    )
```

```python
import math

import jax
import jax.numpy as jnp
from jax import lax
from jax.experimental import pallas as pl
from jax.experimental.pallas import tpu as pltpu
from jax.sharding import PartitionSpec as P

BLOCK = 2048
CHUNKS = 3
MESH = pl.DeviceIdType.MESH


eps_norm = 1e-06
beta_one = 0.9
beta_two = 0.95
adam_eps = 1e-08
learn_rate = 0.01
decay_rate = 0.1
bias_one = 1.0 - 0.9**10
bias_two = 1.0 - 0.95**10


def normalize(tokens, norm_gain):
    wide = tokens.astype(jnp.float32)
    inv_rms = lax.rsqrt(jnp.mean(wide * wide, axis=-1, keepdims=True) + eps_norm)
    normed = (wide * inv_rms * norm_gain).astype(jnp.bfloat16)
    return (wide, inv_rms, normed)


def norm_backward(wide, inv_rms, norm_gain, normed_grad):
    scaled = normed_grad * norm_gain
    inner = jnp.mean(scaled * wide, axis=-1, keepdims=True)
    input_grad = (inv_rms * scaled - wide * inv_rms**3 * inner).astype(jnp.bfloat16)
    gain_term = jnp.sum(normed_grad * wide * inv_rms, axis=0)
    return (input_grad, gain_term)


def rounded(value):
    lowered = lax.optimization_barrier(value.astype(jnp.bfloat16))
    return lowered.astype(jnp.float32)


def decode(codes, table):
    high_part = codes // 16
    low_part = codes - high_part * 16
    levels = lax.broadcasted_iota(jnp.int32, (16, 1, 1), 0)
    pick_low = (low_part[None] == levels).astype(jnp.float32)
    pick_high = (high_part[None] == levels).astype(jnp.float32)
    table_grid = table.reshape(16, 16)
    by_high = jnp.einsum("hl,lrk->hrk", table_grid, pick_low, precision=lax.Precision.HIGHEST)
    return jnp.sum(pick_high * by_high, axis=0)


def adam_update(weight, grad, old_m, old_v):
    first = beta_one * old_m + (1.0 - beta_one) * grad
    second = beta_two * old_v + (1.0 - beta_two) * grad * grad
    direction = first / bias_one / (jnp.sqrt(second / bias_two) + adam_eps)
    new_weight = (
        weight.astype(jnp.float32) * (1.0 - learn_rate * decay_rate) - learn_rate * direction
    ).astype(jnp.bfloat16)
    return (new_weight, first, second)


def block_max(values, row_group):
    blocks = values.reshape(values.shape[0] // row_group, -1)
    return jnp.max(jnp.abs(blocks), axis=1)


def optimize(
    weight, grad, codes_first, codes_second, scales_first, scales_second, qmap_m, qmap_v, row_group
):
    rows, width = weight.shape
    span_rows = math.gcd(rows, 64)
    span_count = rows // span_rows
    per_span = span_rows // row_group

    def one_span(pieces):
        weight_part, grad_part, code_one, code_two, scale_one, scale_two = pieces
        old_m = (
            decode(code_one, qmap_m).reshape(per_span, row_group, width) * scale_one[:, None, None]
        ).reshape(span_rows, width)
        old_v = (
            decode(code_two, qmap_v).reshape(per_span, row_group, width) * scale_two[:, None, None]
        ).reshape(span_rows, width)
        new_part, first, second = adam_update(weight_part, grad_part, old_m, old_v)
        return (new_part, block_max(first, row_group), block_max(second, row_group))

    pieces = (
        weight.reshape(span_count, span_rows, width),
        grad.reshape(span_count, span_rows, width),
        codes_first.reshape(span_count, span_rows, width),
        codes_second.reshape(span_count, span_rows, width),
        scales_first.reshape(span_count, per_span),
        scales_second.reshape(span_count, per_span),
    )
    new_weight, new_first, new_second = lax.map(one_span, pieces)
    return (new_weight.reshape(rows, width), new_first.reshape(-1), new_second.reshape(-1))


def plain_shards(
    tokens, key_cot, norm_gain, key_weight, codes_m, codes_v, scale_m, scale_v, qmap_m, qmap_v
):
    width = key_cot.shape[1]
    row_group = BLOCK // width
    wide, inv_rms, normed = normalize(tokens, norm_gain)
    group_cot = lax.all_gather(key_cot, "shard", axis=0, tiled=True)
    local_cols = jnp.einsum("tk,dk->td", group_cot, key_weight, preferred_element_type=jnp.float32)
    normed_grad = lax.all_to_all(local_cols, "shard", split_axis=0, concat_axis=1, tiled=True)
    input_grad, gain_term = norm_backward(wide, inv_rms, norm_gain, normed_grad)
    gain_grad = lax.psum(gain_term, ("rep", "shard"))
    shard_count = lax.axis_size("shard")
    rep_count = lax.axis_size("rep")
    slice_rows = key_weight.shape[0] // rep_count
    reordered = normed.reshape(normed.shape[0], shard_count, rep_count, slice_rows)
    reordered = reordered.transpose(0, 2, 1, 3).reshape(normed.shape)
    grad = lax.psum_scatter(
        rounded(jnp.einsum("td,tk->dk", reordered, key_cot, preferred_element_type=jnp.float32)),
        ("rep", "shard"),
        scatter_dimension=0,
        tiled=True,
    )
    first_row = lax.axis_index("rep") * slice_rows
    first_block = lax.axis_index("rep") * (slice_rows // row_group)

    def take_rows(array_in):
        return lax.dynamic_slice_in_dim(array_in, first_row, slice_rows, 0)

    def take_blocks(array_in):
        return lax.dynamic_slice_in_dim(array_in, first_block, slice_rows // row_group, 0)

    part_weight, part_m, part_v = optimize(
        take_rows(key_weight),
        grad,
        take_rows(codes_m),
        take_rows(codes_v),
        take_blocks(scale_m),
        take_blocks(scale_v),
        qmap_m,
        qmap_v,
        row_group,
    )
    new_weight = lax.all_gather(part_weight, "rep", axis=0, tiled=True)
    new_scale_m, new_scale_v = (
        lax.all_gather(part_m, "rep", axis=0, tiled=True),
        lax.all_gather(part_v, "rep", axis=0, tiled=True),
    )
    return (input_grad, gain_grad, new_weight, new_scale_m, new_scale_v)


def lookup(codes, table):
    low = codes & 127
    first = jnp.take_along_axis(table[0], low, axis=1)
    second = jnp.take_along_axis(table[1], low, axis=1)
    return jnp.where(codes >= 128, second, first)


def column(values, first, repeat, count):
    row = lax.broadcasted_iota(jnp.int32, (count, 128), 0)
    out = jnp.full((count, 128), values[first], jnp.float32)
    for i in range(1, count // repeat):
        out = jnp.where(row >= i * repeat, values[first + i], out)
    return out


def fused_kernel(
    nr,
    ns,
    tok_hbm,
    cot_ref,
    gain_ref,
    gains,
    w_hbm,
    codes_m,
    codes_v,
    scale_m,
    scale_v,
    table_m,
    table_v,
    ig_ref,
    nw_hbm,
    gain_out,
    scale_out,
    tok_v,
    w_v,
    tok_g,
    cot_g,
    ng,
    ng_home,
    part,
    core_recv,
    red,
    chip_recv,
    nw_own,
    inv_ref,
    gain_own,
    gain_recv,
    gain_sum,
    gain_z,
    scale_own,
    scale_recv,
    held_codes,
    old,
    code_sem,
    loc,
    cot_sem,
    tok_sem,
    ng_sem,
    core_sem,
    chip_sem,
    ag_sem,
    fwd_sem,
    gain_sem,
    gz_sem,
    scale_sem,
):
    rep, shard = lax.axis_index("rep"), lax.axis_index("shard")
    chips = nr // 2
    chip, core = rep // 2, rep % 2
    partner = rep + 1 - 2 * core
    count, features = tok_v.shape
    rows, width = w_v.shape
    span = rows // CHUNKS
    piece = span // nr
    lanes = rows // 128

    def remote(src, dst, sems, slot, **device):
        return pltpu.make_async_remote_copy(
            src_ref=src,
            dst_ref=dst,
            send_sem=sems.at[(0,) + slot],
            recv_sem=sems.at[(1,) + slot],
            device_id=device,
            device_id_type=MESH,
        )

    def next_shard(k):
        return lax.rem(shard + k, ns)

    def next_rep(k):
        return lax.rem(rep + k, nr)

    def next_chip(k):
        return lax.rem(chip + k, chips)

    barrier = pltpu.get_barrier_semaphore()
    for k in range(1, ns):
        pl.semaphore_signal(barrier, inc=1, device_id={"shard": next_shard(k)}, device_id_type=MESH)
    for k in range(1, nr):
        pl.semaphore_signal(barrier, inc=1, device_id={"rep": next_rep(k)}, device_id_type=MESH)

    load_tok = pltpu.make_async_copy(tok_hbm, tok_v, loc.at[0])
    load_tok.start()
    load_w = pltpu.make_async_copy(w_hbm, w_v, loc.at[1])
    load_w.start()
    loads = []
    for i, codes in enumerate((codes_m, codes_v)):
        for c in range(CHUNKS):
            start = pl.multiple_of(c * span + rep * piece, 16)
            loads.append(
                pltpu.make_async_copy(
                    codes.at[pl.ds(start, piece)], held_codes.at[i, c], code_sem.at[i, c]
                )
            )
            loads[-1].start()
    mine = pl.ds(pl.multiple_of(shard * count, count), count)
    own_tok = []
    for c in range(CHUNKS):
        col = pl.multiple_of(shard * rows + c * span, 128)
        own_tok.append(
            pltpu.make_async_copy(
                tok_hbm.at[:, pl.ds(col, span)], tok_g.at[c, mine], loc.at[2 + c]
            )
        )
        own_tok[c].start()
    tok_copies = []
    for c in range(CHUNKS):
        for k in range(1, ns):
            col = pl.multiple_of(next_shard(k) * rows + c * span, 128)
            tok_copies.append(
                remote(
                    tok_hbm.at[:, pl.ds(col, span)],
                    tok_g.at[c, mine],
                    tok_sem,
                    (c, k - 1),
                    shard=next_shard(k),
                )
            )

    def send_tokens(c):
        for k in range(ns - 1):
            tok_copies[c * (ns - 1) + k].start()

    pl.semaphore_wait(barrier, ns - 1 + nr - 1)
    send_tokens(0)
    load_tok.wait()

    @pl.loop(0, count // 16)
    def _(step):
        row = pl.multiple_of(step * 16, 16)
        block = pl.ds(row, 16)
        square = jnp.zeros((16, 128), jnp.float32)
        for col in range(0, features, 128):
            wide = tok_v[block, col : col + 128].astype(jnp.float32)
            square = square + wide * wide
        mean = jnp.sum(square, axis=1, keepdims=True) * (1.0 / features)
        inv = lax.rsqrt(mean + eps_norm)
        inv_ref[block, :] = jnp.broadcast_to(inv, (16, 128))
        scaled = (cot_ref[block, :].astype(jnp.float32) * inv).astype(jnp.bfloat16)
        cot_g[pl.ds(pl.multiple_of(shard * count + row, 16), 16), :] = scaled

    def decode(i):
        table_ref, scale = ((table_m, scale_m), (table_v, scale_v))[i]
        tables = [jnp.broadcast_to(table_ref[k : k + 1, :], (8, 128)) for k in range(2)]
        group = BLOCK // width
        for c in range(CHUNKS):
            loads[i * CHUNKS + c].wait()

            @pl.loop(0, piece // 8)
            def _(step):
                block = pl.ds(pl.multiple_of(step * 8, 8), 8)
                first = (c * span + rep * piece) // group + step * (8 // group)
                factor = column(scale, first, group, 8)
                for col in range(0, width, 128):
                    value = lookup(held_codes[i, c, block, col : col + 128], tables)
                    old[i, c, block, col : col + 128] = value * factor

    def relay(way, t):
        origin = jnp.clip(shard - way * t, 0, ns - 1)
        block = cot_g.at[pl.ds(pl.multiple_of(origin * count, count), count)]
        there = jnp.clip(shard + way, 0, ns - 1)
        return remote(block, block, cot_sem, ((1 - way) // 2, t), shard=there)

    def sends(way, t):
        if way > 0:
            return (shard + 1 < ns) & (shard >= t)
        return (shard >= 1) & (shard + t < ns)

    def takes(way, t):
        return shard >= t + 1 if way > 0 else shard + t + 1 < ns

    for t in range(ns - 1):
        for way in (1, -1):
            if t > 0:

                @pl.when(takes(way, t - 1))
                def _():
                    relay(way, t - 1).wait_recv()

            @pl.when(sends(way, t))
            def _():
                relay(way, t).start()

        if t == 0:
            decode(0)
        elif t == 1:
            send_tokens(1)
            decode(1)
    if ns < 3:
        send_tokens(1)
        decode(1)
    for c in range(2, CHUNKS):
        send_tokens(c)
    for way in (1, -1):

        @pl.when(takes(way, ns - 2))
        def _():
            relay(way, ns - 2).wait_recv()

    load_w.wait()
    own_ng = pltpu.make_async_copy(ng.at[:, mine], ng_home.at[shard], loc.at[2 + CHUNKS])
    ng_copies = []
    for c in range(CHUNKS):
        ng[c] = lax.dot_general(
            cot_g[...],
            w_v[c * span : (c + 1) * span, :],
            (((1,), (1,)), ((), ())),
            preferred_element_type=jnp.float32,
        ).astype(jnp.bfloat16)
        for k in range(1, ns):
            theirs = pl.ds(pl.multiple_of(next_shard(k) * count, count), count)
            ng_copies.append(
                remote(
                    ng.at[c, theirs],
                    ng_home.at[shard, c],
                    ng_sem,
                    (c, k - 1),
                    shard=next_shard(k),
                )
            )
            ng_copies[-1].start()
    own_ng.start()

    core_copies = [
        remote(part.at[c, :, 1 - core], core_recv.at[c], core_sem, (c,), rep=partner)
        for c in range(CHUNKS)
    ]
    chip_copies = [
        [
            remote(
                red.at[c, next_chip(k)],
                chip_recv.at[c, k - 1],
                chip_sem,
                (c, k - 1),
                rep=next_chip(k) * 2 + core,
            )
            for k in range(1, chips)
        ]
        for c in range(CHUNKS)
    ]

    def out_rows(c, owner):
        return pl.ds(pl.multiple_of(c * span + owner * piece, 16), piece)

    ag_copies, fwd_copies, own_nw = [], [], []
    for c in range(CHUNKS):
        here = out_rows(c, rep)
        targets = [next_chip(k) * 2 + core for k in range(1, chips)] + [partner]
        ag_copies.append(
            [
                remote(nw_own.at[c], nw_hbm.at[here], ag_sem, (c, i), rep=target)
                for i, target in enumerate(targets)
            ]
        )
        own_nw.append(
            pltpu.make_async_copy(nw_own.at[c], nw_hbm.at[here], loc.at[3 + CHUNKS + c])
        )
        steps = []
        for k in range(1, chips):
            there = out_rows(c, next_chip(chips - k) * 2 + core)
            steps.append(
                remote(nw_hbm.at[there], nw_hbm.at[there], fwd_sem, (c, k - 1), rep=partner)
            )
        fwd_copies.append(steps)

    def form(c):
        own_tok[c].wait()
        for k in range(ns - 1):
            tok_copies[c * (ns - 1) + k].wait_recv()
        product = lax.dot_general(
            tok_g[c], cot_g[...], (((0,), (0,)), ((), ())), preferred_element_type=jnp.float32
        )
        for j in range(nr):
            part[c, j // 2, j % 2] = product[j * piece : (j + 1) * piece].astype(jnp.bfloat16)
        core_copies[c].start()

        def add(step, total):
            block = pl.ds(pl.multiple_of(step * 32, 32), 32)
            term = ng[c, block, :].astype(jnp.float32) * tok_g[c, block, :].astype(jnp.float32)
            return total + term

        total = lax.fori_loop(
            0, ns * count // 32, add, jnp.zeros((32, span), jnp.float32)
        )
        line = jnp.sum(total, axis=0, keepdims=True)
        for i in range(span // 128):
            k = c * (span // 128) + i
            gain_own[k : k + 1, :] = line[:, i * 128 : (i + 1) * 128]

    def reduce_core(c):
        core_copies[c].wait_recv()
        for q in range(chips):
            both = part[c, q, core].astype(jnp.float32) + core_recv[c, q].astype(jnp.float32)
            red[c, q] = both.astype(jnp.bfloat16)
        for copy in chip_copies[c]:
            copy.start()

    def update(c):
        for copy in chip_copies[c]:
            copy.wait_recv()
        tops = [jnp.zeros((1, 128), jnp.float32)] * 2
        for row in range(0, piece, 16):
            block = slice(row, row + 16)
            grad = red[c, chip, block, :].astype(jnp.float32)
            for k in range(chips - 1):
                grad = grad + chip_recv[c, k, block, :].astype(jnp.float32)
            first_gain = shard * rows + c * span + rep * piece + row
            grad = grad * column(gains, first_gain, 1, 16)[:, 0:1]
            weight = w_v[pl.ds(pl.multiple_of(c * span + rep * piece + row, 16), 16), :]
            new_part, first, second = adam_update(
                weight, grad, old[0, c, block, :], old[1, c, block, :]
            )
            nw_own[c, block, :] = new_part
            place = (
                lax.broadcasted_iota(jnp.int32, (16, 128), 0)
                + row
                - 2 * lax.broadcasted_iota(jnp.int32, (16, 128), 1)
            )
            hit = (place == 0) | (place == 1)
            for i, value in enumerate((jnp.abs(first), second)):
                top = jnp.max(value, axis=1, keepdims=True)
                spread = jnp.where(hit, jnp.broadcast_to(top, (16, 128)), 0.0)
                tops[i] = jnp.maximum(tops[i], jnp.max(spread, axis=0, keepdims=True))
        for copy in ag_copies[c]:
            copy.start()
        own_nw[c].start()
        for i in range(2):
            scale_own[2 * c + i : 2 * c + i + 1, :] = tops[i]

    def forward(c):
        for k in range(chips - 1):
            ag_copies[c][k].wait_recv()
            fwd_copies[c][k].start()

    scale_own[...] = jnp.zeros_like(scale_own)
    gain_own[...] = jnp.zeros_like(gain_own)
    form(0)
    reduce_core(0)
    form(1)
    reduce_core(1)
    update(0)
    form(2)
    gain_copies = [
        remote(gain_own, gain_recv.at[k - 1], gain_sem, (k - 1,), rep=next_rep(k))
        for k in range(1, nr)
    ]
    reduce_core(2)
    for copy in gain_copies:
        copy.start()
    update(1)
    forward(0)
    update(2)
    scale_copies = [
        remote(scale_own, scale_recv.at[rep], scale_sem, (k - 1,), rep=next_rep(k))
        for k in range(1, nr)
    ]
    for copy in scale_copies:
        copy.start()
    scale_recv[rep] = scale_own[...]
    forward(1)
    own_ng.wait()
    for copy in ng_copies:
        copy.wait_recv()

    @pl.loop(0, count // 16)
    def _(step):
        block = pl.ds(pl.multiple_of(step * 16, 16), 16)
        inner = jnp.zeros((16, 128), jnp.float32)
        for col in range(0, features, 128):
            p, c, o = col // rows, col % rows // span, col % span
            scaled = ng_home[p, c, block, o : o + 128].astype(jnp.float32) * gain_ref[:, col : col + 128]
            inner = inner + scaled * tok_v[block, col : col + 128].astype(jnp.float32)
        inv = inv_ref[block, 0:1]
        mean = jnp.sum(inner, axis=1, keepdims=True) * (1.0 / features)
        factor = jnp.broadcast_to(inv * inv * mean, (16, 128))
        for col in range(0, features, 128):
            p, c, o = col // rows, col % rows // span, col % span
            scaled = ng_home[p, c, block, o : o + 128].astype(jnp.float32) * gain_ref[:, col : col + 128]
            wide = tok_v[block, col : col + 128].astype(jnp.float32)
            ig_ref[block, col : col + 128] = (scaled - wide * factor).astype(jnp.bfloat16)

    total = gain_own[...]
    for k in range(nr - 1):
        gain_copies[k].wait_recv()
        total = total + gain_recv[k]
    gain_sum[...] = total
    gz_copies = [
        remote(gain_sum, gain_z.at[shard], gz_sem, (k - 1,), shard=next_shard(k))
        for k in range(1, ns)
    ]
    for copy in gz_copies:
        copy.start()
    gain_z[shard] = total
    forward(2)

    for copy in gz_copies + scale_copies:
        copy.wait_recv()
    gain_out[...] = gain_z[...]
    scale_out[...] = scale_recv[...]
    for c in range(CHUNKS):
        own_nw[c].wait()
        ag_copies[c][chips - 1].wait_recv()
        for copy in fwd_copies[c]:
            copy.wait_recv()
            copy.wait_send()
        for copy in ag_copies[c] + chip_copies[c]:
            copy.wait_send()
        core_copies[c].wait_send()
    for t in range(ns - 1):
        for way in (1, -1):

            @pl.when(sends(way, t))
            def _():
                relay(way, t).wait_send()

    for copy in tok_copies + ng_copies + gain_copies + scale_copies + gz_copies:
        copy.wait_send()


def fused_shards(
    tokens, key_cot, norm_gain, key_weight, codes_m, codes_v, scale_m, scale_v, qmap_m, qmap_v
):
    count, features = tokens.shape
    rows, width = key_weight.shape
    row_group = BLOCK // width
    nr, ns = lax.axis_size("rep"), lax.axis_size("shard")
    span = rows // CHUNKS
    part = span // nr
    chips = nr // 2
    vmem = pl.BlockSpec(memory_space=pltpu.VMEM)
    anywhere = pl.BlockSpec(memory_space=pl.ANY)
    smem = pl.BlockSpec(memory_space=pltpu.SMEM)
    lanes = -(-rows // 1024) * 8
    levels = -(-2 * CHUNKS // 8) * 8
    half, full = jnp.bfloat16, jnp.float32
    dma = pltpu.SemaphoreType.DMA
    input_grad, new_weight, gain_tiles, scale_tiles = pl.pallas_call(
        lambda *refs: fused_kernel(nr, ns, *refs),
        out_shape=(
            jax.ShapeDtypeStruct((count, features), half),
            jax.ShapeDtypeStruct((rows, width), half),
            jax.ShapeDtypeStruct((ns, lanes, 128), full),
            jax.ShapeDtypeStruct((nr, levels, 128), full),
        ),
        in_specs=[anywhere, vmem, vmem, smem] + [anywhere] * 3 + [smem] * 2 + [vmem] * 2,
        out_specs=(vmem, anywhere, vmem, vmem),
        scratch_shapes=[
            pltpu.VMEM((count, features), half),
            pltpu.VMEM((rows, width), half),
            pltpu.VMEM((CHUNKS, ns * count, span), half),
            pltpu.VMEM((ns * count, width), half),
            pltpu.VMEM((CHUNKS, ns * count, span), half),
            pltpu.VMEM((ns, CHUNKS, count, span), half),
            pltpu.VMEM((CHUNKS, chips, 2, part, width), half),
            pltpu.VMEM((CHUNKS, chips, part, width), half),
            pltpu.VMEM((CHUNKS, chips, part, width), half),
            pltpu.VMEM((CHUNKS, chips - 1, part, width), half),
            pltpu.VMEM((CHUNKS, part, width), half),
            pltpu.VMEM((count, 128), full),
            pltpu.VMEM((lanes, 128), full),
            pltpu.VMEM((nr - 1, lanes, 128), full),
            pltpu.VMEM((lanes, 128), full),
            pltpu.VMEM((ns, lanes, 128), full),
            pltpu.VMEM((levels, 128), full),
            pltpu.VMEM((nr, levels, 128), full),
            pltpu.VMEM((2, CHUNKS, part, width), jnp.int32),
            pltpu.VMEM((2, CHUNKS, part, width), full),
            dma((2, CHUNKS)),
            dma((3 + 2 * CHUNKS,)),
            dma((2, 2, ns - 1)),
            dma((2, CHUNKS, ns - 1)),
            dma((2, CHUNKS, ns - 1)),
            dma((2, CHUNKS)),
            dma((2, CHUNKS, chips - 1)),
            dma((2, CHUNKS, chips)),
            dma((2, CHUNKS, chips - 1)),
            dma((2, nr - 1)),
            dma((2, ns - 1)),
            dma((2, nr - 1)),
        ],
        compiler_params=pltpu.CompilerParams(
            collective_id=0, has_side_effects=True, vmem_limit_bytes=60 * 2**20
        ),
        cost_estimate=pl.CostEstimate(
            flops=4 * ns * count * rows * width, bytes_accessed=12 * 2**20, transcendentals=0
        ),
        name="fused",
    )(
        tokens,
        key_cot,
        norm_gain.reshape(1, features),
        norm_gain,
        key_weight,
        codes_m,
        codes_v,
        scale_m,
        scale_v,
        qmap_m.reshape(2, 128),
        qmap_v.reshape(2, 128),
    )
    gain_grad = gain_tiles[:, : rows // 128].reshape(features)
    maxima = scale_tiles[:, : 2 * CHUNKS, : part // row_group]
    maxima = maxima.reshape(nr, CHUNKS, 2, part // row_group).transpose(2, 1, 0, 3).reshape(2, -1)
    return (input_grad, gain_grad, new_weight, maxima[0], maxima[1])


def shards(tokens, key_cot, norm_gain, key_weight, *rest):
    part = key_weight.shape[0] // CHUNKS // lax.axis_size("rep")
    even = (
        key_weight.shape[0] % (CHUNKS * 128) == 0
        and part % 16 == 0
        and lax.axis_size("rep") % 2 == 0
        and key_cot.shape[1] * 2 == BLOCK
    )
    body = fused_shards if even else plain_shards
    return body(tokens, key_cot, norm_gain, key_weight, *rest)


def solution(mesh):
    placed = (
        P(("rep", "shard"), None),
        P(("rep", "shard"), None),
        P(),
        P("shard", None),
        P("shard", None),
        P("shard", None),
        P("shard"),
        P("shard"),
        P(),
        P(),
    )
    return jax.shard_map(
        shards,
        mesh=mesh,
        in_specs=placed,
        out_specs=(P(("rep", "shard"), None), P(), P("shard", None), P("shard"), P("shard")),
        check_vma=False,
    )
```
